32 devices in a mesh: gx: 8 (over z, y), gy: 4 (over x, core).
Axes of the slice: x: 2, y: 2, z: 4, core: 2. Of those that a mesh axis runs over, the one named last changes fastest.
Arguments:
- cell_means: float32 [30, 32, 16, 128], P(None, 'gx', 'gy'), may hold values from 0 to 1
- diffusion: float32 [32, 16, 128], P('gx', 'gy'), may hold values from 0.02 to 0.15
- mix_rate: float32 [32, 16, 128], P('gx', 'gy'), may hold values from 0.05 to 3
- send_lists: int32 [32, 32, 128], P(('gx', 'gy')), may hold values from 0 to 2047
- compositions: float32 [30, 131072], P(None, ('gx', 'gy')), may hold values from 0 to 1
- weights: float32 [131072], P(('gx', 'gy')), may hold values from 0.5 to 2
- particle_slots: int32 [131072], P(('gx', 'gy')), may hold values from 0 to 4095
- partners: int32 [131072], P(('gx', 'gy')), may hold values from 0 to 4095
Outputs:
- new_means: float32 [30, 32, 16, 128], P(None, 'gx', 'gy')
- new_compositions: float32 [30, 131072], P(None, ('gx', 'gy'))
The draws below stay inside these ranges and needn't reach their ends.
Inputs may be any that keep to these rules, and one draw needn't show every extreme that they name: particle_slots = s * 128 + r names slot r of the list that tile s sends to the particle's device.
All inputs are finite; a program needn't handle non-finite values.
Results may differ from the reference program's by a relative error of at most 0.00002.
Values sent between devices are 32-bit elements; how exact they have to be, the bound alone decides.
A program may use at most 64 MiB of HBM per device.

```python
import math
import jax
import jax.numpy as jnp
import numpy as np

SPECIES = 30
CX = 4
CY = 4
CZ = 128
SLOTS = 128
P_DEV = 4096
NX = 32
NY = 16
PARTS_SIZE = 131072
N_GX = 8
N_GY = 4


def place_ends(drawn, own_key, smallest, largest):
    longest = drawn.shape.index(max(drawn.shape))
    spots = []
    for shift in (0, 1):
        where = [jax.random.randint(jax.random.fold_in(own_key, axis), (), 0, length) for axis, length in enumerate(drawn.shape)]
        where[longest] = (where[longest] + shift) % drawn.shape[longest]
        spots.append(tuple(where))
    return drawn.at[spots[0]].set(smallest).at[spots[1]].set(largest)


def block_scale(stream_key, shape, shards, low, largest):
    factor_of = 1.0
    for axis_at, shards_of in shards:
        steps = jax.random.uniform(jax.random.fold_in(jax.random.fold_in(stream_key, 6), axis_at), (shards_of,), jnp.float32, low / len(shards), largest / len(shards))
        factor_of = factor_of * jnp.repeat(jnp.exp(steps), shape[axis_at] // shards_of).reshape((-1,) + (1,) * (len(shape) - 1 - axis_at))
    return factor_of


def rank_bounds(amount, skew):
    loads = [(1 << 20) // math.isqrt(grade ** skew) + 1 for grade in range(1, amount + 1)]
    deviation = 1 + sum(loads) // (1 << 30)
    return np.cumsum(np.array([max(1, weight // deviation) for weight in loads]))


def ranked_ids(key, extent, number_of, skew):
    listing = rank_bounds(number_of, skew)
    ticket = jax.random.randint(jax.random.fold_in(key, 1), extent, 0, int(listing[number_of - 1]))
    rank = jnp.searchsorted(jnp.asarray(listing, jnp.int32), ticket, side="right")
    return jax.random.permutation(jax.random.fold_in(key, 2), number_of)[rank].astype(jnp.int32)


def setup_inputs(seed: int = 0) -> dict:
    keys = jax.random.split(jax.random.key(seed), 9)
    return {
        "cell_means": jnp.clip(1.0 * jax.random.uniform(keys[0], (SPECIES, NX, NY, CZ), jnp.float32) ** block_scale(keys[0], (SPECIES, NX, NY, CZ), ((1, 8), (2, 4)), -0.2, 0.2), 0.0, 1.0),
        "diffusion": jnp.clip(0.02 + 0.13000001 * jax.random.uniform(keys[1], (NX, NY, CZ), jnp.float32) ** block_scale(keys[1], (NX, NY, CZ), ((0, 8), (1, 4)), -0.2, 0.2), 0.02, 0.15),
        "mix_rate": jnp.clip(jnp.exp(math.log(3.0) - 4.0943445 * jax.random.uniform(keys[2], (NX, NY, CZ), jnp.float32) ** block_scale(keys[2], (NX, NY, CZ), ((0, 8), (1, 4)), -0.2, 0.2)), 0.05, 3.0),
        "send_lists": place_ends(jax.random.randint(keys[3], (N_GX * N_GY, N_GX * N_GY, SLOTS), 0, CX * CY * CZ), jax.random.fold_in(keys[3], 1), 0, (CX * CY * CZ) - 1).astype(jnp.int32),
        "compositions": jnp.clip(1.0 * jax.random.uniform(keys[4], (SPECIES, PARTS_SIZE), jnp.float32) ** block_scale(keys[4], (SPECIES, PARTS_SIZE), ((1, 32),), -0.2, 0.2), 0.0, 1.0),
        "weights": jnp.clip(jnp.exp(math.log(2.0) - 1.3862944 * jax.random.uniform(keys[5], (PARTS_SIZE,), jnp.float32) ** block_scale(keys[5], (PARTS_SIZE,), ((0, 32),), -0.2, 0.2)), 0.5, 2.0),
        "particle_slots": place_ends(ranked_ids(keys[6], (PARTS_SIZE,), N_GX * N_GY * SLOTS, 1), jax.random.fold_in(keys[6], 3), 0, (N_GX * N_GY * SLOTS) - 1).astype(jnp.int32),
        "partners": place_ends(jax.random.randint(keys[7], (PARTS_SIZE,), 0, P_DEV), jax.random.fold_in(keys[7], 1), 0, P_DEV - 1).astype(jnp.int32),
    }


PAIR_RATE = 0.3


def reference(cell_means, diffusion, mix_rate, send_lists, compositions, weights, particle_slots, partners):
    devices = N_GX * N_GY
    cell_count = CX * CY * CZ
    padded = jnp.pad(cell_means, ((0, 0), (1, 1), (1, 1), (1, 1)))
    neighbours = padded[:, 2:, 1:-1, 1:-1] + padded[:, :-2, 1:-1, 1:-1]
    neighbours = neighbours + padded[:, 1:-1, 2:, 1:-1] + padded[:, 1:-1, :-2, 1:-1]
    neighbours = neighbours + padded[:, 1:-1, 1:-1, 2:] + padded[:, 1:-1, 1:-1, :-2]
    filtered = cell_means + diffusion[None] * (neighbours - 6.0 * cell_means)
    fields = jnp.concatenate([filtered, mix_rate[None]], 0)
    blocks = fields.reshape(SPECIES + 1, N_GX, CX, N_GY, CY, CZ).transpose(1, 3, 2, 4, 5, 0)
    blocks = blocks.reshape(devices * cell_count, SPECIES + 1)
    owner = (jnp.arange(devices * P_DEV) // P_DEV).astype(jnp.int32)
    source = (particle_slots // SLOTS).astype(jnp.int32)
    within = (particle_slots % SLOTS).astype(jnp.int32)
    target = source * cell_count + send_lists[source, owner, within]
    local_means = blocks[target].T
    blend_rate = 1.0 - jnp.exp(-local_means[SPECIES])
    mates = compositions[:, owner * P_DEV + partners]
    new_compositions = compositions - blend_rate[None] * (compositions - local_means[:SPECIES]) - PAIR_RATE * (compositions - mates)
    weighted = jnp.concatenate([weights[None] * new_compositions, weights[None]], 0)
    totals = jax.ops.segment_sum(weighted.T, target, num_segments=devices * cell_count)
    updated = (totals[:, :SPECIES] + blocks[:, :SPECIES]) / (totals[:, SPECIES:] + 1.0)
    new_means = updated.reshape(N_GX, N_GY, CX, CY, CZ, SPECIES).transpose(5, 0, 2, 1, 3, 4)
    new_means = new_means.reshape(SPECIES, NX, NY, CZ)
    return new_means, new_compositions
```

```python
import functools

import jax
import jax.numpy as jnp
from jax import lax
from jax.experimental import pallas as pl
from jax.experimental.pallas import tpu as pltpu
from jax.sharding import PartitionSpec as P

PAIR_RATE = 0.3
LANES = 128
ROWS = 32
GROUPS = ROWS // 8
F32 = jnp.float32
BF16 = jnp.bfloat16


def pick(table, count, index, start=0, sums=None):
    lane = jnp.broadcast_to(index & (LANES - 1), (8, LANES))
    chunk = jnp.broadcast_to(index >> 7, (8, LANES))
    if sums is None:
        sums = tuple(jnp.zeros((8, LANES), F32) for _ in range(GROUPS))

    def step(at, sums):
        mask = chunk == at
        return tuple(
            jnp.where(
                mask,
                jnp.take_along_axis(
                    table[at, 8 * g : 8 * g + 8, :], lane, axis=1, mode="promise_in_bounds"
                ),
                total,
            )
            for g, total in enumerate(sums)
        )

    return lax.fori_loop(start, start + count, step, sums, unroll=min(count, 16))


def stencil(cells, halo, diffusion, fields, rows_x, rows_y):
    lane = lax.broadcasted_iota(jnp.int32, (ROWS, LANES), 1)
    for x in range(rows_x):
        for y in range(rows_y):
            mid = cells[x, y]
            total = cells[x + 1, y] if x + 1 < rows_x else halo[1, y]
            total = total + (cells[x - 1, y] if x else halo[0, y])
            total = total + (cells[x, y + 1] if y + 1 < rows_y else halo[3, x])
            total = total + (cells[x, y - 1] if y else halo[2, x])
            total = total + jnp.where(lane < LANES - 1, pltpu.roll(mid, LANES - 1, 1), 0.0)
            total = total + jnp.where(lane > 0, pltpu.roll(mid, 1, 1), 0.0)
            j = x * rows_y + y
            fields[j] = mid + diffusion[j : j + 1, :] * (total - 6.0 * mid)


def split_store(values, high, low, at):
    first = values.astype(BF16)
    high[:, pl.ds(at, LANES)] = first
    low[:, pl.ds(at, LANES)] = (values - first.astype(F32)).astype(BF16)


def scatter_block(index, high, low, left, acc, groups, first):
    width = index.shape[1]
    group = (index >> 8).astype(F32).astype(BF16)
    group = jnp.broadcast_to(group, (ROWS, width))
    for g in range(groups):
        mask = group == jnp.array(g, BF16)
        zero = jnp.zeros((ROWS, width), BF16)
        left[2 * g * ROWS : (2 * g + 1) * ROWS, :] = jnp.where(mask, high, zero)
        left[(2 * g + 1) * ROWS : (2 * g + 2) * ROWS, :] = jnp.where(mask, low, zero)
    place = lax.broadcasted_iota(jnp.int32, (256, width), 0)
    right = jnp.where(place == (index & 255), 1.0, 0.0).astype(BF16)
    part = lax.dot_general(
        left[...], right, (((1,), (1,)), ((), ())), preferred_element_type=F32
    )
    if first:
        acc[...] = part
    else:
        acc[...] += part


def acc_row(acc, j):
    g, half = j // 2, (j % 2) * LANES
    return (
        acc[2 * g * ROWS : (2 * g + 1) * ROWS, half : half + LANES]
        + acc[(2 * g + 1) * ROWS : (2 * g + 2) * ROWS, half : half + LANES]
    )


def load_cells(means, cells, rows_x, rows_y):
    species = means.shape[0] // (rows_x * rows_y)
    for x in range(rows_x):
        for y in range(rows_y):
            j = x * rows_y + y
            cells[x, y, 0:species, :] = means[pl.ds(j, species, stride=rows_x * rows_y), :]
            cells[x, y, species:ROWS, :] = jnp.zeros((ROWS - species, LANES), F32)


def send_kernel(rows_x, rows_y, means, halo, diffusion, rate, lists, fields, outgoing, cells):
    species = means.shape[0] // (rows_x * rows_y)
    load_cells(means, cells, rows_x, rows_y)
    stencil(cells, halo, diffusion, fields, rows_x, rows_y)
    count = rows_x * rows_y
    blend = 1.0 - jnp.exp(-rate[...])
    for j in range(count):
        fields[j, species : species + 1, :] = blend[j : j + 1, :]

    def body(d, _):
        parts = pick(fields, count, lists[pl.ds(d, 1), :])
        for g in range(GROUPS):
            outgoing[d, 8 * g : 8 * g + 8, :] = parts[g]
        return 0

    lax.fori_loop(0, lists.shape[0], body, 0)


def mates_kernel(compositions, partners, mates, table):
    species = compositions.shape[0]
    count = compositions.shape[1] // LANES
    for b in range(count):
        table[b, 0:species, :] = compositions[:, b * LANES : (b + 1) * LANES]
        table[b, species:ROWS, :] = jnp.zeros((ROWS - species, LANES), F32)

    def body(b, _):
        parts = pick(table, count, partners[pl.ds(b, 1), :])
        for g in range(GROUPS):
            rows = slice(8 * g, 8 * g + 8)
            mine = table[b, rows, :]
            mates[b, rows, :] = PAIR_RATE * (mine - parts[g])
        return 0

    lax.fori_loop(0, count, body, 0)


def mix_kernel(compositions, received, pair, weights, slots, new, moments, high, low, left, acc):
    species = compositions.shape[0]
    blocks = slots.shape[0]
    chunks = received.shape[0]

    def body(b, _):
        at = pl.multiple_of(b * LANES, LANES)
        parts = pick(received, chunks, slots[pl.ds(b, 1), :])
        local = jnp.concatenate(parts, 0)
        mine = compositions[:, pl.ds(at, LANES)]
        fresh = mine - local[species : species + 1] * (mine - local[:species])
        fresh = fresh - pair[b, 0:species, :]
        new[:, pl.ds(at, LANES)] = fresh
        weight = weights[pl.ds(b, 1), :]
        values = jnp.concatenate(
            [weight * fresh, weight, jnp.zeros((ROWS - species - 1, LANES), F32)], 0
        )
        split_store(values, high, low, at)
        return 0

    lax.fori_loop(0, blocks, body, 0)
    per = left.shape[1] // LANES
    for k in range(blocks // per):
        index = jnp.concatenate([slots[k * per + i : k * per + i + 1, :] for i in range(per)], 1)
        cols = slice(k * per * LANES, (k + 1) * per * LANES)
        scatter_block(index, high[:, cols], low[:, cols], left, acc, chunks // 2, k == 0)
    for s in range(chunks):
        moments[s] = acc_row(acc, s)


def means_kernel(returned, lists, fields, out, high, low, left, acc):
    blocks, count = returned.shape[0], fields.shape[0]
    species = out.shape[0] // count
    for b in range(blocks):
        split_store(returned[b], high, low, b * LANES)
    per = left.shape[1] // LANES
    for k in range(blocks // per):
        index = jnp.concatenate([lists[k * per + i : k * per + i + 1, :] for i in range(per)], 1)
        cols = slice(k * per * LANES, (k + 1) * per * LANES)
        scatter_block(index, high[:, cols], low[:, cols], left, acc, count // 2, k == 0)
    for j in range(count):
        total = acc_row(acc, j)
        mean = (total[:species] + fields[j, 0:species, :]) / (total[species : species + 1] + 1.0)
        out[pl.ds(j, species, stride=count), :] = mean


def call(kernel, name, out_shape, scratch, *args):
    return pl.pallas_call(
        kernel,
        out_shape=out_shape,
        name=name,
        scratch_shapes=scratch,
        compiler_params=pltpu.CompilerParams(vmem_limit_bytes=40 * 1024 * 1024),
    )(*args)


def shift(block, axis, up):
    n = lax.axis_size(axis)
    pairs = [(i, i + 1) if up else (i + 1, i) for i in range(n - 1)]
    return lax.ppermute(block, axis, pairs)


def on_device(
    cell_means, diffusion, mix_rate, send_lists, compositions, weights, particle_slots, partners
):
    species, rows_x, rows_y, depth = cell_means.shape
    count = rows_x * rows_y
    tiles = send_lists.shape[1]
    particles = compositions.shape[1]
    blocks = particles // LANES
    sds = lambda *shape: jax.ShapeDtypeStruct(shape, F32)
    halo = jnp.stack(
        [
            shift(cell_means[:, -1], "gx", True),
            shift(cell_means[:, 0], "gx", False),
            shift(cell_means[:, :, -1], "gy", True),
            shift(cell_means[:, :, 0], "gy", False),
        ]
    ).transpose(0, 2, 1, 3)
    halo = jnp.pad(halo, ((0, 0), (0, 0), (0, ROWS - species), (0, 0)))
    lists = send_lists[0]
    fields, outgoing = call(
        functools.partial(send_kernel, rows_x, rows_y),
        "send_kernel",
        (sds(count, ROWS, LANES), sds(tiles, ROWS, LANES)),
        [pltpu.VMEM((rows_x, rows_y, ROWS, LANES), F32)],
        cell_means.reshape(species * count, depth),
        halo,
        diffusion.reshape(count, depth),
        mix_rate.reshape(count, depth),
        lists,
    )
    received = lax.all_to_all(outgoing, ("gx", "gy"), split_axis=0, concat_axis=0, tiled=True)
    pair = call(
        mates_kernel,
        "mates_kernel",
        sds(blocks, ROWS, LANES),
        [pltpu.VMEM((blocks, ROWS, LANES), F32)],
        compositions,
        partners.reshape(blocks, LANES),
    )
    width = 512
    new, moments = call(
        mix_kernel,
        "mix_kernel",
        (sds(species, particles), sds(tiles, ROWS, LANES)),
        [
            pltpu.VMEM((ROWS, particles), BF16),
            pltpu.VMEM((ROWS, particles), BF16),
            pltpu.VMEM((tiles * ROWS, width), BF16),
            pltpu.VMEM((tiles * ROWS, 256), F32),
        ],
        compositions,
        received,
        pair,
        weights.reshape(blocks, LANES),
        particle_slots.reshape(blocks, LANES),
    )
    returned = lax.all_to_all(moments, ("gx", "gy"), split_axis=0, concat_axis=0, tiled=True)
    out = call(
        means_kernel,
        "means_kernel",
        sds(species * count, LANES),
        [
            pltpu.VMEM((ROWS, tiles * LANES), BF16),
            pltpu.VMEM((ROWS, tiles * LANES), BF16),
            pltpu.VMEM((count * ROWS, width), BF16),
            pltpu.VMEM((count * ROWS, 256), F32),
        ],
        returned,
        lists,
        fields,
    )
    return out.reshape(species, rows_x, rows_y, depth), new


def solution(mesh):
    in_specs = (
        P(None, "gx", "gy", None),
        P("gx", "gy", None),
        P("gx", "gy", None),
        P(("gx", "gy"), None, None),
        P(None, ("gx", "gy")),
        P(("gx", "gy")),
        P(("gx", "gy")),
        P(("gx", "gy")),
    )
    out_specs = (P(None, "gx", "gy", None), P(None, ("gx", "gy")))
    return jax.shard_map(
        on_device, mesh=mesh, in_specs=in_specs, out_specs=out_specs, check_vma=False
    )
```

```python
import functools

import jax
import jax.numpy as jnp
from jax import lax
from jax.experimental import pallas as pl
from jax.experimental.pallas import tpu as pltpu
from jax.sharding import PartitionSpec as P

PAIR_RATE = 0.3
LANES = 128
ROWS = 32
GROUPS = ROWS // 8
F32 = jnp.float32
BF16 = jnp.bfloat16


def pick(table, count, index, start=0, sums=None):
    lane = jnp.broadcast_to(index & (LANES - 1), (8, LANES))
    chunk = jnp.broadcast_to(index >> 7, (8, LANES))
    if sums is None:
        sums = tuple(jnp.zeros((8, LANES), F32) for _ in range(GROUPS))

    def step(at, sums):
        mask = chunk == at
        return tuple(
            jnp.where(
                mask,
                jnp.take_along_axis(
                    table[at, 8 * g : 8 * g + 8, :], lane, axis=1, mode="promise_in_bounds"
                ),
                total,
            )
            for g, total in enumerate(sums)
        )

    return lax.fori_loop(start, start + count, step, sums, unroll=min(count, 16))


def stencil(cells, halo, diffusion, fields, rows_x, rows_y):
    lane = lax.broadcasted_iota(jnp.int32, (ROWS, LANES), 1)
    for x in range(rows_x):
        for y in range(rows_y):
            mid = cells[x, y]
            total = cells[x + 1, y] if x + 1 < rows_x else halo[1, y]
            total = total + (cells[x - 1, y] if x else halo[0, y])
            total = total + (cells[x, y + 1] if y + 1 < rows_y else halo[3, x])
            total = total + (cells[x, y - 1] if y else halo[2, x])
            total = total + jnp.where(lane < LANES - 1, pltpu.roll(mid, LANES - 1, 1), 0.0)
            total = total + jnp.where(lane > 0, pltpu.roll(mid, 1, 1), 0.0)
            j = x * rows_y + y
            fields[j] = mid + diffusion[j : j + 1, :] * (total - 6.0 * mid)


def scatter_block(index, high, low, left, acc, groups):
    width = index.shape[1]
    group = (index >> 8).astype(F32).astype(BF16)
    group = jnp.broadcast_to(group, (ROWS, width))
    for g in range(groups):
        mask = group == jnp.array(g, BF16)
        zero = jnp.zeros((ROWS, width), BF16)
        left[2 * g * ROWS : (2 * g + 1) * ROWS, :] = jnp.where(mask, high, zero)
        left[(2 * g + 1) * ROWS : (2 * g + 2) * ROWS, :] = jnp.where(mask, low, zero)
    place = lax.broadcasted_iota(jnp.int32, (256, width), 0)
    right = jnp.where(place == (index & 255), 1.0, 0.0).astype(BF16)
    part = lax.dot_general(
        left[...], right, (((1,), (1,)), ((), ())), preferred_element_type=F32
    )
    acc[...] += part


def acc_row(acc, j):
    g, half = j // 2, (j % 2) * LANES
    return (
        acc[2 * g * ROWS : (2 * g + 1) * ROWS, half : half + LANES]
        + acc[(2 * g + 1) * ROWS : (2 * g + 2) * ROWS, half : half + LANES]
    )


def load_cells(means, cells, rows_x, rows_y):
    species = means.shape[0] // (rows_x * rows_y)
    for x in range(rows_x):
        for y in range(rows_y):
            j = x * rows_y + y
            cells[x, y, 0:species, :] = means[pl.ds(j, species, stride=rows_x * rows_y), :]
            cells[x, y, species:ROWS, :] = jnp.zeros((ROWS - species, LANES), F32)


def gather_pairs(compositions, partners, table, parts, pair):
    species, particles = compositions.shape
    groups = particles // 256
    for h in range(groups):
        values = compositions[:, h * 256 : (h + 1) * 256]
        values = jnp.concatenate([values, jnp.zeros((ROWS - species, 256), F32)], 0)
        first = values.astype(BF16)
        table[h * ROWS : (h + 1) * ROWS, 0:256] = first
        table[h * ROWS : (h + 1) * ROWS, 256:512] = (values - first.astype(F32)).astype(BF16)

    def body(k, _):
        index = jnp.concatenate([partners[pl.ds(2 * k + i, 1), :] for i in range(2)], 1)
        place = lax.broadcasted_iota(jnp.int32, (256, 256), 0)
        hot = jnp.where(place == (index & 255), 1.0, 0.0).astype(BF16)
        hot = jnp.concatenate([hot, hot], 0)
        parts[...] = jnp.dot(table[...], hot, preferred_element_type=F32)
        group = jnp.broadcast_to(index >> 8, (ROWS, 256))
        total = jnp.zeros((ROWS, 256), F32)
        for h in range(groups):
            total = jnp.where(group == h, parts[h * ROWS : (h + 1) * ROWS, :], total)
        at = pl.multiple_of(k * 256, 256)
        pair[0:species, pl.ds(at, 256)] = PAIR_RATE * (
            compositions[:, pl.ds(at, 256)] - total[:species]
        )
        return 0

    lax.fori_loop(0, particles // 256, body, 0)


def whole_kernel(
    nx, ny, rows_x, rows_y,
    means, diffusion, rate, lists, compositions, weights, slots, partners,
    out, new,
    cells, halo, fields, outgoing, received, local, moments, returned,
    table, parts, pair, high, low, left1, acc1, left2, acc2,
    halo_send, halo_recv, go_send, go_recv, back_send, back_recv,
):
    tiles = nx * ny
    half = tiles // 2
    count = rows_x * rows_y
    species = compositions.shape[0]
    blocks = slots.shape[0]
    gx, gy = lax.axis_index("gx"), lax.axis_index("gy")
    me = gx * ny + gy

    def place(d):
        return (lax.div(d, ny), lax.rem(d, ny))

    barrier = pltpu.get_barrier_semaphore()

    def greet(k, _):
        d = lax.rem(me + k, tiles)
        pl.semaphore_signal(
            barrier, inc=1, device_id=place(d), device_id_type=pl.DeviceIdType.MESH
        )
        return 0

    lax.fori_loop(1, tiles, greet, 0)

    for x in range(rows_x):
        for y in range(rows_y):
            j = x * rows_y + y
            cells[x, y, 0:species, :] = means[pl.ds(j, species, stride=count), :]
            cells[x, y, species:ROWS, :] = jnp.zeros((ROWS - species, LANES), F32)

    pl.semaphore_wait(barrier, tiles - 1)

    def halo_copy(i):
        source, length, target = (
            (cells.at[rows_x - 1], rows_y, (gx + 1, gy)),
            (cells.at[0], rows_y, (gx - 1, gy)),
            (cells.at[:, rows_y - 1], rows_x, (gx, gy + 1)),
            (cells.at[:, 0], rows_x, (gx, gy - 1)),
        )[i]
        return pltpu.make_async_remote_copy(
            src_ref=source,
            dst_ref=halo.at[i, 0:length],
            send_sem=halo_send.at[i],
            recv_sem=halo_recv.at[i],
            device_id=target,
            device_id_type=pl.DeviceIdType.MESH,
        )

    sends = (gx < nx - 1, gx > 0, gy < ny - 1, gy > 0)
    receives = (gx > 0, gx < nx - 1, gy > 0, gy < ny - 1)
    for i in range(4):

        @pl.when(sends[i])
        def _(i=i):
            halo_copy(i).start()

        @pl.when(jnp.logical_not(receives[i]))
        def _(i=i):
            halo[i] = jnp.zeros(halo.shape[1:], F32)

    gather_pairs(compositions, partners, table, parts, pair)

    for i in range(4):

        @pl.when(receives[i])
        def _(i=i):
            halo_copy(i).wait_recv()

    stencil(cells, halo, diffusion, fields, rows_x, rows_y)
    blend = 1.0 - jnp.exp(-rate[...])
    for j in range(count):
        fields[j, species : species + 1, :] = blend[j : j + 1, :]

    def copy_of(buffers, sems, source, d, target):
        return pltpu.make_async_remote_copy(
            src_ref=buffers[0].at[d],
            dst_ref=buffers[1].at[source],
            send_sem=sems[0].at[d],
            recv_sem=sems[1].at[source],
            device_id=place(target),
            device_id_type=pl.DeviceIdType.MESH,
        )

    go = (outgoing, received), (go_send, go_recv)
    back = (moments, returned), (back_send, back_recv)

    def fill(d, buffer, row):
        found = pick(fields, count, lists[pl.ds(d, 1), :])
        for g in range(GROUPS):
            buffer[row, 8 * g : 8 * g + 8, :] = found[g]

    def send_one(k):
        d = lax.rem(me + k, tiles)
        fill(d, outgoing, d)
        copy_of(*go, me, d, d).start()

    lax.fori_loop(0, half, lambda i, _: (send_one(half + i), 0)[1], 0)
    lax.fori_loop(1, half, lambda i, _: (send_one(half - i), 0)[1], 0)
    fill(me, received, me)

    def source_of(k):
        return lax.rem(me + tiles - k, tiles)

    def wait_for(which, k):
        @pl.when(k > 0)
        def _():
            s = source_of(k)
            copy_of(*which, s, s, s).wait_recv()

    step_of = 8

    def arrivals(first_k, sign):
        def batch(n, _):
            ks = [first_k + sign * (n * step_of + i) for i in range(step_of)]
            for k in ks:
                wait_for(go, k)

            def body(b, _):
                index = slots[pl.ds(b, 1), :]
                lane = jnp.broadcast_to(index & (LANES - 1), (8, LANES))
                chunk = jnp.broadcast_to(index >> 7, (8, LANES))
                sums = [local[b, 8 * g : 8 * g + 8, :] for g in range(GROUPS)]
                for k in ks:
                    s = source_of(k)
                    mask = chunk == s
                    for g in range(GROUPS):
                        rows = received[s, 8 * g : 8 * g + 8, :]
                        found = jnp.take_along_axis(
                            rows, lane, axis=1, mode="promise_in_bounds"
                        )
                        sums[g] = jnp.where(mask, found, sums[g])
                for g in range(GROUPS):
                    local[b, 8 * g : 8 * g + 8, :] = sums[g]
                return 0

            lax.fori_loop(0, blocks, body, 0, unroll=2)
            return 0

        lax.fori_loop(0, half // step_of, batch, 0)

    local[...] = jnp.zeros(local.shape, F32)
    arrivals(half, 1)
    arrivals(half - 1, -1)

    def mix(b, _):
        at = pl.multiple_of(b * LANES, LANES)
        mine = compositions[:, pl.ds(at, LANES)]
        fresh = mine - local[b, species : species + 1, :] * (mine - local[b, 0:species, :])
        fresh = fresh - pair[0:species, pl.ds(at, LANES)]
        new[:, pl.ds(at, LANES)] = fresh
        weight = weights[pl.ds(b, 1), :]
        values = jnp.concatenate(
            [weight * fresh, weight, jnp.zeros((ROWS - species - 1, LANES), F32)], 0
        )
        first = values.astype(BF16)
        high[:, pl.ds(at, LANES)] = first
        low[:, pl.ds(at, LANES)] = (values - first.astype(F32)).astype(BF16)
        return 0

    lax.fori_loop(0, blocks, mix, 0, unroll=2)
    acc1[...] = jnp.zeros(acc1.shape, F32)
    per = left1.shape[1] // LANES

    def gather_moments(k, _):
        index = jnp.concatenate([slots[pl.ds(k * per + i, 1), :] for i in range(per)], 1)
        at = pl.multiple_of(k * per * LANES, per * LANES)
        cols = pl.ds(at, per * LANES)
        scatter_block(index, high[:, cols], low[:, cols], left1, acc1, half)
        return 0

    lax.fori_loop(0, blocks // per, gather_moments, 0)
    for s in range(tiles):
        moments[s] = acc_row(acc1, s)

    def return_one(k):
        d = lax.rem(me + k, tiles)
        copy_of(*back, me, d, d).start()

    lax.fori_loop(0, half, lambda i, _: (return_one(half + i), 0)[1], 0)
    lax.fori_loop(1, half, lambda i, _: (return_one(half - i), 0)[1], 0)
    returned[me] = moments[me]

    acc2[...] = jnp.zeros(acc2.shape, F32)
    per2 = left2.shape[1] // LANES

    def returns(first_k, sign):
        def batch(n, _):
            ks = [first_k + sign * (n * per2 + i) for i in range(per2)]
            for k in ks:
                wait_for(back, k)
            values = jnp.concatenate([returned[source_of(k)] for k in ks], 1)
            index = jnp.concatenate([lists[pl.ds(source_of(k), 1), :] for k in ks], 1)
            first = values.astype(BF16)
            second = (values - first.astype(F32)).astype(BF16)
            scatter_block(index, first, second, left2, acc2, count // 2)
            return 0

        lax.fori_loop(0, half // per2, batch, 0)

    returns(half, 1)
    returns(half - 1, -1)
    for j in range(count):
        total = acc_row(acc2, j)
        mean = (total[:species] + fields[j, 0:species, :]) / (total[species : species + 1] + 1.0)
        out[pl.ds(j, species, stride=count), :] = mean

    for i in range(4):

        @pl.when(sends[i])
        def _(i=i):
            halo_copy(i).wait_send()

    def finish(k, _):
        d = lax.rem(me + k, tiles)
        copy_of(*go, me, d, d).wait_send()
        copy_of(*back, me, d, d).wait_send()
        return 0

    lax.fori_loop(1, tiles, finish, 0)


def on_device(
    cell_means, diffusion, mix_rate, send_lists, compositions, weights, particle_slots, partners
):
    species, rows_x, rows_y, depth = cell_means.shape
    count = rows_x * rows_y
    tiles = send_lists.shape[1]
    particles = compositions.shape[1]
    blocks = particles // LANES
    width = 512
    vmem = lambda *shape: pltpu.VMEM(shape, F32)
    half_vmem = lambda *shape: pltpu.VMEM(shape, BF16)
    out, new = pl.pallas_call(
        functools.partial(
            whole_kernel, lax.axis_size("gx"), lax.axis_size("gy"), rows_x, rows_y
        ),
        out_shape=(
            jax.ShapeDtypeStruct((species * count, LANES), F32),
            jax.ShapeDtypeStruct((species, particles), F32),
        ),
        in_specs=[pl.BlockSpec(memory_space=pltpu.VMEM)] * 8,
        out_specs=[pl.BlockSpec(memory_space=pltpu.VMEM)] * 2,
        name="whole_kernel",
        scratch_shapes=[
            vmem(rows_x, rows_y, ROWS, LANES),
            vmem(4, max(rows_x, rows_y), ROWS, LANES),
            vmem(count, ROWS, LANES),
            vmem(tiles, ROWS, LANES),
            vmem(tiles, ROWS, LANES),
            vmem(blocks, ROWS, LANES),
            vmem(tiles, ROWS, LANES),
            vmem(tiles, ROWS, LANES),
            half_vmem(particles // 256 * ROWS, 512),
            vmem(particles // 256 * ROWS, 256),
            vmem(ROWS, particles),
            half_vmem(ROWS, particles),
            half_vmem(ROWS, particles),
            half_vmem(tiles * ROWS, width),
            vmem(tiles * ROWS, 256),
            half_vmem(count * ROWS, width),
            vmem(count * ROWS, 256),
            pltpu.SemaphoreType.DMA((4,)),
            pltpu.SemaphoreType.DMA((4,)),
            pltpu.SemaphoreType.DMA((tiles,)),
            pltpu.SemaphoreType.DMA((tiles,)),
            pltpu.SemaphoreType.DMA((tiles,)),
            pltpu.SemaphoreType.DMA((tiles,)),
        ],
        compiler_params=pltpu.CompilerParams(
            collective_id=0, has_side_effects=True, vmem_limit_bytes=44 * 1024 * 1024
        ),
    )(
        cell_means.reshape(species * count, depth),
        diffusion.reshape(count, depth),
        mix_rate.reshape(count, depth),
        send_lists[0],
        compositions,
        weights.reshape(blocks, LANES),
        particle_slots.reshape(blocks, LANES),
        partners.reshape(blocks, LANES),
    )
    return out.reshape(species, rows_x, rows_y, depth), new


def solution(mesh):
    in_specs = (
        P(None, "gx", "gy", None),
        P("gx", "gy", None),
        P("gx", "gy", None),
        P(("gx", "gy"), None, None),
        P(None, ("gx", "gy")),
        P(("gx", "gy")),
        P(("gx", "gy")),
        P(("gx", "gy")),
    )
    out_specs = (P(None, "gx", "gy", None), P(None, ("gx", "gy")))
    return jax.shard_map(
        on_device, mesh=mesh, in_specs=in_specs, out_specs=out_specs, check_vma=False
    )
```

```python
import functools

import jax
import jax.numpy as jnp
from jax import lax
from jax.experimental import pallas as pl
from jax.experimental.pallas import tpu as pltpu
from jax.sharding import PartitionSpec as P

PAIR_RATE = 0.3
LANES = 128
ROWS = 32
GROUPS = ROWS // 8
PLANE = 8
F32 = jnp.float32
BF16 = jnp.bfloat16


def pick(table, count, index, start=0, sums=None):
    lane = jnp.broadcast_to(index & (LANES - 1), (8, LANES))
    chunk = jnp.broadcast_to(index >> 7, (8, LANES))
    if sums is None:
        sums = tuple(jnp.zeros((8, LANES), F32) for _ in range(GROUPS))

    def step(at, sums):
        mask = chunk == at
        return tuple(
            jnp.where(
                mask,
                jnp.take_along_axis(
                    table[at, 8 * g : 8 * g + 8, :], lane, axis=1, mode="promise_in_bounds"
                ),
                total,
            )
            for g, total in enumerate(sums)
        )

    return lax.fori_loop(start, start + count, step, sums, unroll=min(count, 16))


def stencil(cells, halo, diffusion, fields, rows_x, rows_y):
    lane = lax.broadcasted_iota(jnp.int32, (ROWS, LANES), 1)
    for x in range(rows_x):
        for y in range(rows_y):
            mid = cells[x, y]
            total = cells[x + 1, y] if x + 1 < rows_x else halo[1, y]
            total = total + (cells[x - 1, y] if x else halo[0, y])
            total = total + (cells[x, y + 1] if y + 1 < rows_y else halo[3, x])
            total = total + (cells[x, y - 1] if y else halo[2, x])
            total = total + jnp.where(lane < LANES - 1, pltpu.roll(mid, LANES - 1, 1), 0.0)
            total = total + jnp.where(lane > 0, pltpu.roll(mid, 1, 1), 0.0)
            j = x * rows_y + y
            fields[j] = mid + diffusion[j : j + 1, :] * (total - 6.0 * mid)


def scatter_block(group, hot, high, low, left, acc, groups):
    width = group.shape[1]
    group = jnp.broadcast_to(group.astype(F32).astype(BF16), (ROWS, width))
    for g in range(groups):
        mask = group == jnp.array(g, BF16)
        zero = jnp.zeros((ROWS, width), BF16)
        left[2 * g * ROWS : (2 * g + 1) * ROWS, :] = jnp.where(mask, high, zero)
        left[(2 * g + 1) * ROWS : (2 * g + 2) * ROWS, :] = jnp.where(mask, low, zero)
    acc[...] += lax.dot_general(
        left[...], hot, (((1,), (1,)), ((), ())), preferred_element_type=F32
    )


def hot_rows(index):
    place = lax.broadcasted_iota(jnp.int32, (256, index.shape[1]), 0)
    return jnp.where(place == (index & 255), 1.0, 0.0).astype(BF16)


def acc_row(acc, j):
    g, half = j // 2, (j % 2) * LANES
    return (
        acc[2 * g * ROWS : (2 * g + 1) * ROWS, half : half + LANES]
        + acc[(2 * g + 1) * ROWS : (2 * g + 2) * ROWS, half : half + LANES]
    )


def load_cells(means, cells, rows_x, rows_y):
    species = means.shape[0] // (rows_x * rows_y)
    for x in range(rows_x):
        for y in range(rows_y):
            j = x * rows_y + y
            cells[x, y, 0:species, :] = means[pl.ds(j, species, stride=rows_x * rows_y), :]
            cells[x, y, species:ROWS, :] = jnp.zeros((ROWS - species, LANES), F32)


def gather_pairs(compositions, partners, table, parts, pair):
    species, particles = compositions.shape
    groups = particles // 256
    for h in range(groups):
        values = compositions[:, h * 256 : (h + 1) * 256]
        values = jnp.concatenate([values, jnp.zeros((ROWS - species, 256), F32)], 0)
        first = values.astype(BF16)
        table[h * ROWS : (h + 1) * ROWS, 0:256] = first
        table[h * ROWS : (h + 1) * ROWS, 256:512] = (values - first.astype(F32)).astype(BF16)

    def body(k, _):
        index = jnp.concatenate([partners[pl.ds(2 * k + i, 1), :] for i in range(2)], 1)
        place = lax.broadcasted_iota(jnp.int32, (256, 256), 0)
        hot = jnp.where(place == (index & 255), 1.0, 0.0).astype(BF16)
        hot = jnp.concatenate([hot, hot], 0)
        parts[...] = jnp.dot(table[...], hot, preferred_element_type=F32)
        group = jnp.broadcast_to(index >> 8, (ROWS, 256))
        total = jnp.zeros((ROWS, 256), F32)
        for h in range(groups):
            total = jnp.where(group == h, parts[h * ROWS : (h + 1) * ROWS, :], total)
        at = pl.multiple_of(k * 256, 256)
        pair[0:species, pl.ds(at, 256)] = PAIR_RATE * (
            compositions[:, pl.ds(at, 256)] - total[:species]
        )
        return 0

    lax.fori_loop(0, particles // 256, body, 0)


def whole_kernel(
    nx, ny, rows_x, rows_y, *refs
):
    inputs, (out, new_out), refs = refs[:8], refs[8:10], refs[10:]
    staged, refs = refs[:8], refs[8:]
    means, diffusion, rate, lists, compositions, weights, slots, partners = staged
    (
        new, cells, halo, fields, outgoing, received, local, moments, returned,
        table, parts, pair, high, low, hot1, left1, acc1, left2, acc2,
        in_sems, out_sem, halo_send, halo_recv, go_send, go_recv, back_send, back_recv,
    ) = refs
    tiles = nx * ny
    planes = tiles // PLANE
    count = rows_x * rows_y
    species = compositions.shape[0]
    blocks = slots.shape[0]
    gx, gy = lax.axis_index("gx"), lax.axis_index("gy")
    me = gx * ny + gy
    plane, inner = lax.div(me, PLANE), lax.rem(me, PLANE)

    def place(d):
        return (lax.div(d, ny), lax.rem(d, ny))

    loads = [
        pltpu.make_async_copy(inputs[i], staged[i], in_sems.at[i]) for i in range(8)
    ]
    for i in (0, 1, 2, 4, 7, 3, 6, 5):
        loads[i].start()

    barrier = pltpu.get_barrier_semaphore()

    def greet(k, _):
        d = lax.rem(me + k, tiles)
        pl.semaphore_signal(
            barrier, inc=1, device_id=place(d), device_id_type=pl.DeviceIdType.MESH
        )
        return 0

    lax.fori_loop(1, tiles, greet, 0)

    loads[0].wait()
    for x in range(rows_x):
        for y in range(rows_y):
            j = x * rows_y + y
            cells[x, y, 0:species, :] = means[pl.ds(j, species, stride=count), :]
            cells[x, y, species:ROWS, :] = jnp.zeros((ROWS - species, LANES), F32)

    pl.semaphore_wait(barrier, tiles - 1)

    def halo_copy(i):
        source, length, target = (
            (cells.at[rows_x - 1], rows_y, (gx + 1, gy)),
            (cells.at[0], rows_y, (gx - 1, gy)),
            (cells.at[:, rows_y - 1], rows_x, (gx, gy + 1)),
            (cells.at[:, 0], rows_x, (gx, gy - 1)),
        )[i]
        return pltpu.make_async_remote_copy(
            src_ref=source,
            dst_ref=halo.at[i, 0:length],
            send_sem=halo_send.at[i],
            recv_sem=halo_recv.at[i],
            device_id=target,
            device_id_type=pl.DeviceIdType.MESH,
        )

    sends = (gx < nx - 1, gx > 0, gy < ny - 1, gy > 0)
    receives = (gx > 0, gx < nx - 1, gy > 0, gy < ny - 1)
    for i in range(4):

        @pl.when(sends[i])
        def _(i=i):
            halo_copy(i).start()

        @pl.when(jnp.logical_not(receives[i]))
        def _(i=i):
            halo[i] = jnp.zeros(halo.shape[1:], F32)

    loads[4].wait()
    loads[7].wait()
    gather_pairs(compositions, partners, table, parts, pair)
    for i in (1, 2, 3, 5, 6):
        loads[i].wait()
    for b in range(0, blocks, 4):
        index = jnp.concatenate([slots[b + i : b + i + 1, :] for i in range(4)], 1)
        hot1[:, b * LANES : (b + 4) * LANES] = hot_rows(index)
    local[...] = jnp.zeros(local.shape, F32)

    for i in range(4):

        @pl.when(receives[i])
        def _(i=i):
            halo_copy(i).wait_recv()

    stencil(cells, halo, diffusion, fields, rows_x, rows_y)
    blend = 1.0 - jnp.exp(-rate[...])
    for j in range(count):
        fields[j, species : species + 1, :] = blend[j : j + 1, :]

    def copy_of(buffers, sems, source, d, target):
        return pltpu.make_async_remote_copy(
            src_ref=buffers[0].at[d, 0 : species + 1],
            dst_ref=buffers[1].at[source, 0 : species + 1],
            send_sem=sems[0].at[d],
            recv_sem=sems[1].at[source],
            device_id=place(target),
            device_id_type=pl.DeviceIdType.MESH,
        )

    go = (outgoing, received), (go_send, go_recv)
    back = (moments, returned), (back_send, back_recv)

    def fill(d, buffer, row):
        found = pick(fields, count, lists[pl.ds(d, 1), :])
        for g in range(GROUPS):
            buffer[row, 8 * g : 8 * g + 8, :] = found[g]

    def send_plane(there, first):
        def body(i, _):
            d = there * PLANE + lax.rem(inner + i, PLANE)
            fill(d, outgoing, d)
            copy_of(*go, me, d, d).start()
            return 0

        lax.fori_loop(first, PLANE, body, 0)

    def far_first(step):
        half = planes // 2
        lax.fori_loop(half, planes, lambda k, _: (step(k), 0)[1], 0)
        lax.fori_loop(1, half, lambda k, _: (step(half - k), 0)[1], 0)

    far_first(lambda k: send_plane(lax.rem(plane + k, planes), 0))
    fill(me, received, me)
    send_plane(plane, 1)

    def wait_plane(which, there, first):
        def body(i, _):
            s = there * PLANE + lax.rem(inner + i, PLANE)
            copy_of(*which, s, s, s).wait_recv()
            return 0

        lax.fori_loop(first, PLANE, body, 0)

    per = left1.shape[1]

    def work(there, first):
        wait_plane(go, there, first)

        def body(b, _):
            index = slots[pl.ds(b, 1), :]
            lane = jnp.broadcast_to(index & (LANES - 1), (8, LANES))
            chunk = jnp.broadcast_to((index >> 7) - there * PLANE, (8, LANES))
            sums = [local[b, 8 * g : 8 * g + 8, :] for g in range(GROUPS)]
            for i in range(PLANE):
                mask = chunk == i
                for g in range(GROUPS):
                    rows = received[there * PLANE + i, 8 * g : 8 * g + 8, :]
                    found = jnp.take_along_axis(rows, lane, axis=1, mode="promise_in_bounds")
                    sums[g] = jnp.where(mask, found, sums[g])
            for g in range(GROUPS):
                local[b, 8 * g : 8 * g + 8, :] = sums[g]
            at = pl.multiple_of(b * LANES, LANES)
            cell = jnp.concatenate(sums, 0)
            mine = compositions[:, pl.ds(at, LANES)]
            fresh = mine - cell[species : species + 1, :] * (mine - cell[:species, :])
            fresh = fresh - pair[0:species, pl.ds(at, LANES)]
            new[:, pl.ds(at, LANES)] = fresh
            weight = weights[pl.ds(b, 1), :]
            values = jnp.concatenate(
                [weight * fresh, weight, jnp.zeros((ROWS - species - 1, LANES), F32)], 0
            )
            top = values.astype(BF16)
            high[:, pl.ds(at, LANES)] = top
            low[:, pl.ds(at, LANES)] = (values - top.astype(F32)).astype(BF16)
            return 0

        lax.fori_loop(0, blocks, body, 0, unroll=2)
        acc1[...] = jnp.zeros(acc1.shape, F32)

        def scatter(k, _):
            rows = [slots[pl.ds(k * (per // LANES) + i, 1), :] for i in range(per // LANES)]
            group = (jnp.concatenate(rows, 1) >> 8) - there * (PLANE // 2)
            cols = pl.ds(pl.multiple_of(k * per, per), per)
            scatter_block(
                group, hot1[:, cols], high[:, cols], low[:, cols], left1, acc1, PLANE // 2
            )
            return 0

        lax.fori_loop(0, blocks * LANES // per, scatter, 0)
        for i in range(PLANE):
            moments[there * PLANE + i] = acc_row(acc1, i)

        def body_back(i, _):
            d = there * PLANE + lax.rem(inner + i, PLANE)
            copy_of(*back, me, d, d).start()
            return 0

        lax.fori_loop(first, PLANE, body_back, 0)

    far_first(lambda k: work(lax.rem(plane + planes - k, planes), 0))
    work(plane, 1)
    store = pltpu.make_async_copy(new, new_out, out_sem)
    store.start()
    returned[me] = moments[me]

    acc2[...] = jnp.zeros(acc2.shape, F32)

    def collect(there, first):
        wait_plane(back, there, first)
        at = [there * PLANE + i for i in range(PLANE)]
        values = jnp.concatenate([returned[s] for s in at], 1)
        index = jnp.concatenate([lists[pl.ds(s, 1), :] for s in at], 1)
        top = values.astype(BF16)
        rest = (values - top.astype(F32)).astype(BF16)
        scatter_block(index >> 8, hot_rows(index), top, rest, left2, acc2, count // 2)

    far_first(lambda k: collect(lax.rem(plane + k, planes), 0))
    collect(plane, 1)
    for j in range(count):
        total = acc_row(acc2, j)
        mean = (total[:species] + fields[j, 0:species, :]) / (total[species : species + 1] + 1.0)
        out[pl.ds(j, species, stride=count), :] = mean

    for i in range(4):

        @pl.when(sends[i])
        def _(i=i):
            halo_copy(i).wait_send()

    def finish(k, _):
        d = lax.rem(me + k, tiles)
        copy_of(*go, me, d, d).wait_send()
        copy_of(*back, me, d, d).wait_send()
        return 0

    lax.fori_loop(1, tiles, finish, 0)
    store.wait()


def on_device(
    cell_means, diffusion, mix_rate, send_lists, compositions, weights, particle_slots, partners
):
    species, rows_x, rows_y, depth = cell_means.shape
    count = rows_x * rows_y
    tiles = send_lists.shape[1]
    particles = compositions.shape[1]
    blocks = particles // LANES
    vmem = lambda *shape: pltpu.VMEM(shape, F32)
    half_vmem = lambda *shape: pltpu.VMEM(shape, BF16)
    operands = (
        cell_means.reshape(species * count, depth),
        diffusion.reshape(count, depth),
        mix_rate.reshape(count, depth),
        send_lists[0],
        compositions,
        weights.reshape(blocks, LANES),
        particle_slots.reshape(blocks, LANES),
        partners.reshape(blocks, LANES),
    )
    out, new = pl.pallas_call(
        functools.partial(
            whole_kernel, lax.axis_size("gx"), lax.axis_size("gy"), rows_x, rows_y
        ),
        out_shape=(
            jax.ShapeDtypeStruct((species * count, LANES), F32),
            jax.ShapeDtypeStruct((species, particles), F32),
        ),
        in_specs=[pl.BlockSpec(memory_space=pltpu.HBM)] * 8,
        out_specs=[
            pl.BlockSpec(memory_space=pltpu.VMEM),
            pl.BlockSpec(memory_space=pltpu.HBM),
        ],
        name="whole_kernel",
        scratch_shapes=[pltpu.VMEM(a.shape, a.dtype) for a in operands]
        + [
            vmem(species, particles),
            vmem(rows_x, rows_y, ROWS, LANES),
            vmem(4, max(rows_x, rows_y), ROWS, LANES),
            vmem(count, ROWS, LANES),
            vmem(tiles, ROWS, LANES),
            vmem(tiles, ROWS, LANES),
            vmem(blocks, ROWS, LANES),
            vmem(tiles, ROWS, LANES),
            vmem(tiles, ROWS, LANES),
            half_vmem(particles // 256 * ROWS, 512),
            vmem(particles // 256 * ROWS, 256),
            vmem(ROWS, particles),
            half_vmem(ROWS, particles),
            half_vmem(ROWS, particles),
            half_vmem(256, particles),
            half_vmem(PLANE * ROWS, 1024),
            vmem(PLANE * ROWS, 256),
            half_vmem(count * ROWS, PLANE * LANES),
            vmem(count * ROWS, 256),
            pltpu.SemaphoreType.DMA((8,)),
            pltpu.SemaphoreType.DMA,
            pltpu.SemaphoreType.DMA((4,)),
            pltpu.SemaphoreType.DMA((4,)),
            pltpu.SemaphoreType.DMA((tiles,)),
            pltpu.SemaphoreType.DMA((tiles,)),
            pltpu.SemaphoreType.DMA((tiles,)),
            pltpu.SemaphoreType.DMA((tiles,)),
        ],
        compiler_params=pltpu.CompilerParams(
            collective_id=0, has_side_effects=True, vmem_limit_bytes=63 * 1024 * 1024
        ),
    )(*operands)
    return out.reshape(species, rows_x, rows_y, depth), new


def solution(mesh):
    in_specs = (
        P(None, "gx", "gy", None),
        P("gx", "gy", None),
        P("gx", "gy", None),
        P(("gx", "gy"), None, None),
        P(None, ("gx", "gy")),
        P(("gx", "gy")),
        P(("gx", "gy")),
        P(("gx", "gy")),
    )
    out_specs = (P(None, "gx", "gy", None), P(None, ("gx", "gy")))
    return jax.shard_map(
        on_device, mesh=mesh, in_specs=in_specs, out_specs=out_specs, check_vma=False
    )
```

```python
import functools

import jax
import jax.numpy as jnp
from jax import lax
from jax.experimental import pallas as pl
from jax.experimental.pallas import tpu as pltpu
from jax.sharding import PartitionSpec as P

PAIR_RATE = 0.3
LANES = 128
ROWS = 32
GROUPS = ROWS // 8
PLANE = 8
F32 = jnp.float32
BF16 = jnp.bfloat16


def pick(table, count, index, start=0, sums=None):
    lane = jnp.broadcast_to(index & (LANES - 1), (8, LANES))
    chunk = jnp.broadcast_to(index >> 7, (8, LANES))
    if sums is None:
        sums = tuple(jnp.zeros((8, LANES), F32) for _ in range(GROUPS))

    def step(at, sums):
        mask = chunk == at
        return tuple(
            jnp.where(
                mask,
                jnp.take_along_axis(
                    table[at, 8 * g : 8 * g + 8, :], lane, axis=1, mode="promise_in_bounds"
                ),
                total,
            )
            for g, total in enumerate(sums)
        )

    return lax.fori_loop(start, start + count, step, sums, unroll=min(count, 16))


def stencil(cells, halo, diffusion, fields, rows_x, rows_y):
    lane = lax.broadcasted_iota(jnp.int32, (ROWS, LANES), 1)
    for x in range(rows_x):
        for y in range(rows_y):
            mid = cells[x, y]
            total = cells[x + 1, y] if x + 1 < rows_x else halo[1, y]
            total = total + (cells[x - 1, y] if x else halo[0, y])
            total = total + (cells[x, y + 1] if y + 1 < rows_y else halo[3, x])
            total = total + (cells[x, y - 1] if y else halo[2, x])
            total = total + jnp.where(lane < LANES - 1, pltpu.roll(mid, LANES - 1, 1), 0.0)
            total = total + jnp.where(lane > 0, pltpu.roll(mid, 1, 1), 0.0)
            j = x * rows_y + y
            fields[j] = mid + diffusion[j : j + 1, :] * (total - 6.0 * mid)


def scatter_block(group, hot, high, low, left, acc, groups):
    width = group.shape[1]
    group = jnp.broadcast_to(group.astype(F32).astype(BF16), (ROWS, width))
    for g in range(groups):
        mask = group == jnp.array(g, BF16)
        zero = jnp.zeros((ROWS, width), BF16)
        left[2 * g * ROWS : (2 * g + 1) * ROWS, :] = jnp.where(mask, high, zero)
        left[(2 * g + 1) * ROWS : (2 * g + 2) * ROWS, :] = jnp.where(mask, low, zero)
    acc[...] += lax.dot_general(
        left[...], hot, (((1,), (1,)), ((), ())), preferred_element_type=F32
    )


def hot_rows(index):
    place = lax.broadcasted_iota(jnp.int32, (256, index.shape[1]), 0)
    return jnp.where(place == (index & 255), 1.0, 0.0).astype(BF16)


def acc_row(acc, j):
    g, half = j // 2, (j % 2) * LANES
    return (
        acc[2 * g * ROWS : (2 * g + 1) * ROWS, half : half + LANES]
        + acc[(2 * g + 1) * ROWS : (2 * g + 2) * ROWS, half : half + LANES]
    )


def load_cells(means, cells, rows_x, rows_y):
    species = means.shape[0] // (rows_x * rows_y)
    for x in range(rows_x):
        for y in range(rows_y):
            j = x * rows_y + y
            cells[x, y, 0:species, :] = means[pl.ds(j, species, stride=rows_x * rows_y), :]
            cells[x, y, species:ROWS, :] = jnp.zeros((ROWS - species, LANES), F32)


def gather_pairs(compositions, partners, table, parts, pair):
    species, particles = compositions.shape
    groups = particles // 256
    for h in range(groups):
        values = compositions[:, h * 256 : (h + 1) * 256]
        values = jnp.concatenate([values, jnp.zeros((ROWS - species, 256), F32)], 0)
        first = values.astype(BF16)
        table[h * ROWS : (h + 1) * ROWS, 0:256] = first
        table[h * ROWS : (h + 1) * ROWS, 256:512] = (values - first.astype(F32)).astype(BF16)

    def body(k, _):
        index = jnp.concatenate([partners[pl.ds(2 * k + i, 1), :] for i in range(2)], 1)
        place = lax.broadcasted_iota(jnp.int32, (256, 256), 0)
        hot = jnp.where(place == (index & 255), 1.0, 0.0).astype(BF16)
        hot = jnp.concatenate([hot, hot], 0)
        parts[...] = jnp.dot(table[...], hot, preferred_element_type=F32)
        group = jnp.broadcast_to(index >> 8, (ROWS, 256))
        total = jnp.zeros((ROWS, 256), F32)
        for h in range(groups):
            total = jnp.where(group == h, parts[h * ROWS : (h + 1) * ROWS, :], total)
        at = pl.multiple_of(k * 256, 256)
        pair[0:species, pl.ds(at, 256)] = PAIR_RATE * (
            compositions[:, pl.ds(at, 256)] - total[:species]
        )
        return 0

    lax.fori_loop(0, particles // 256, body, 0)


def whole_kernel(
    nx, ny, rows_x, rows_y, *refs
):
    inputs, (out, new_out), refs = refs[:8], refs[8:10], refs[10:]
    staged, refs = refs[:8], refs[8:]
    means, diffusion, rate, lists, compositions, weights, slots, partners = staged
    (
        new, cells, halo, fields, outgoing, received, local, moments, returned,
        table, parts, pair, high, low, hot1, left1, acc1, left2, acc2,
        in_sems, out_sem, halo_send, halo_recv, go_send, go_recv, back_send, back_recv,
    ) = refs
    tiles = nx * ny
    planes = tiles // PLANE
    count = rows_x * rows_y
    species = compositions.shape[0]
    blocks = slots.shape[0]
    gx, gy = lax.axis_index("gx"), lax.axis_index("gy")
    me = gx * ny + gy
    plane, inner = lax.div(me, PLANE), lax.rem(me, PLANE)

    def place(d):
        return (lax.div(d, ny), lax.rem(d, ny))

    loads = [
        pltpu.make_async_copy(inputs[i], staged[i], in_sems.at[i]) for i in range(8)
    ]
    for i in (0, 1, 2, 4, 7, 3, 6, 5):
        loads[i].start()

    barrier = pltpu.get_barrier_semaphore()

    def greet(k, _):
        d = lax.rem(me + k, tiles)
        pl.semaphore_signal(
            barrier, inc=1, device_id=place(d), device_id_type=pl.DeviceIdType.MESH
        )
        return 0

    lax.fori_loop(1, tiles, greet, 0)

    loads[0].wait()
    for x in range(rows_x):
        for y in range(rows_y):
            j = x * rows_y + y
            cells[x, y, 0:species, :] = means[pl.ds(j, species, stride=count), :]
            cells[x, y, species:ROWS, :] = jnp.zeros((ROWS - species, LANES), F32)

    pl.semaphore_wait(barrier, tiles - 1)

    def halo_copy(i):
        source, length, target = (
            (cells.at[rows_x - 1], rows_y, (gx + 1, gy)),
            (cells.at[0], rows_y, (gx - 1, gy)),
            (cells.at[:, rows_y - 1], rows_x, (gx, gy + 1)),
            (cells.at[:, 0], rows_x, (gx, gy - 1)),
        )[i]
        return pltpu.make_async_remote_copy(
            src_ref=source,
            dst_ref=halo.at[i, 0:length],
            send_sem=halo_send.at[i],
            recv_sem=halo_recv.at[i],
            device_id=target,
            device_id_type=pl.DeviceIdType.MESH,
        )

    sends = (gx < nx - 1, gx > 0, gy < ny - 1, gy > 0)
    receives = (gx > 0, gx < nx - 1, gy > 0, gy < ny - 1)
    for i in range(4):

        @pl.when(sends[i])
        def _(i=i):
            halo_copy(i).start()

        @pl.when(jnp.logical_not(receives[i]))
        def _(i=i):
            halo[i] = jnp.zeros(halo.shape[1:], F32)

    loads[4].wait()
    loads[7].wait()
    gather_pairs(compositions, partners, table, parts, pair)
    for i in (1, 2, 3, 5, 6):
        loads[i].wait()
    for b in range(0, blocks, 4):
        index = jnp.concatenate([slots[b + i : b + i + 1, :] for i in range(4)], 1)
        hot1[:, b * LANES : (b + 4) * LANES] = hot_rows(index)
    local[...] = jnp.zeros(local.shape, F32)

    for i in range(4):

        @pl.when(receives[i])
        def _(i=i):
            halo_copy(i).wait_recv()

    stencil(cells, halo, diffusion, fields, rows_x, rows_y)
    blend = 1.0 - jnp.exp(-rate[...])
    for j in range(count):
        fields[j, species : species + 1, :] = blend[j : j + 1, :]

    def copy_of(buffers, sems, source, d, target):
        return pltpu.make_async_remote_copy(
            src_ref=buffers[0].at[d, 0 : species + 1],
            dst_ref=buffers[1].at[source, 0 : species + 1],
            send_sem=sems[0].at[d],
            recv_sem=sems[1].at[source],
            device_id=place(target),
            device_id_type=pl.DeviceIdType.MESH,
        )

    go = (outgoing, received), (go_send, go_recv)
    back = (moments, returned), (back_send, back_recv)

    def fill(d, buffer, row):
        found = pick(fields, count, lists[pl.ds(d, 1), :])
        for g in range(GROUPS):
            buffer[row, 8 * g : 8 * g + 8, :] = found[g]

    def send_plane(there, first):
        def body(i, _):
            d = there * PLANE + lax.rem(inner + i, PLANE)
            fill(d, outgoing, d)
            copy_of(*go, me, d, d).start()
            return 0

        lax.fori_loop(first, PLANE, body, 0)

    def far_first(step):
        half = planes // 2
        lax.fori_loop(half, planes, lambda k, _: (step(k), 0)[1], 0)
        lax.fori_loop(1, half, lambda k, _: (step(half - k), 0)[1], 0)

    far_first(lambda k: send_plane(lax.rem(plane + k, planes), 0))
    fill(me, received, me)
    send_plane(plane, 1)

    def wait_plane(which, there, first):
        def body(i, _):
            s = there * PLANE + lax.rem(inner + i, PLANE)
            copy_of(*which, s, s, s).wait_recv()
            return 0

        lax.fori_loop(first, PLANE, body, 0)

    per = left1.shape[1]

    def work(there, first):
        wait_plane(go, there, first)

        def body(b, _):
            index = slots[pl.ds(b, 1), :]
            lane = jnp.broadcast_to(index & (LANES - 1), (8, LANES))
            chunk = jnp.broadcast_to((index >> 7) - there * PLANE, (8, LANES))
            sums = [local[b, 8 * g : 8 * g + 8, :] for g in range(GROUPS)]
            for i in range(PLANE):
                mask = chunk == i
                for g in range(GROUPS):
                    rows = received[there * PLANE + i, 8 * g : 8 * g + 8, :]
                    found = jnp.take_along_axis(rows, lane, axis=1, mode="promise_in_bounds")
                    sums[g] = jnp.where(mask, found, sums[g])
            for g in range(GROUPS):
                local[b, 8 * g : 8 * g + 8, :] = sums[g]
            at = pl.multiple_of(b * LANES, LANES)
            cell = jnp.concatenate(sums, 0)
            mine = compositions[:, pl.ds(at, LANES)]
            fresh = mine - cell[species : species + 1, :] * (mine - cell[:species, :])
            fresh = fresh - pair[0:species, pl.ds(at, LANES)]
            new[:, pl.ds(at, LANES)] = fresh
            weight = weights[pl.ds(b, 1), :]
            values = jnp.concatenate(
                [weight * fresh, weight, jnp.zeros((ROWS - species - 1, LANES), F32)], 0
            )
            top = values.astype(BF16)
            high[:, pl.ds(at, LANES)] = top
            low[:, pl.ds(at, LANES)] = (values - top.astype(F32)).astype(BF16)
            return 0

        lax.fori_loop(0, blocks, body, 0, unroll=4)
        acc1[...] = jnp.zeros(acc1.shape, F32)

        def scatter(k, _):
            rows = [slots[pl.ds(k * (per // LANES) + i, 1), :] for i in range(per // LANES)]
            group = (jnp.concatenate(rows, 1) >> 8) - there * (PLANE // 2)
            cols = pl.ds(pl.multiple_of(k * per, per), per)
            scatter_block(
                group, hot1[:, cols], high[:, cols], low[:, cols], left1, acc1, PLANE // 2
            )
            return 0

        lax.fori_loop(0, blocks * LANES // per, scatter, 0)
        for i in range(PLANE):
            moments[there * PLANE + i] = acc_row(acc1, i)

        def body_back(i, _):
            d = there * PLANE + lax.rem(inner + i, PLANE)
            copy_of(*back, me, d, d).start()
            return 0

        lax.fori_loop(first, PLANE, body_back, 0)

    far_first(lambda k: work(lax.rem(plane + planes - k, planes), 0))
    work(plane, 1)
    store = pltpu.make_async_copy(new, new_out, out_sem)
    store.start()
    returned[me] = moments[me]

    acc2[...] = jnp.zeros(acc2.shape, F32)

    def collect(there, first):
        wait_plane(back, there, first)
        at = [there * PLANE + i for i in range(PLANE)]
        values = jnp.concatenate([returned[s] for s in at], 1)
        index = jnp.concatenate([lists[pl.ds(s, 1), :] for s in at], 1)
        top = values.astype(BF16)
        rest = (values - top.astype(F32)).astype(BF16)
        scatter_block(index >> 8, hot_rows(index), top, rest, left2, acc2, count // 2)

    far_first(lambda k: collect(lax.rem(plane + k, planes), 0))
    collect(plane, 1)
    for j in range(count):
        total = acc_row(acc2, j)
        mean = (total[:species] + fields[j, 0:species, :]) / (total[species : species + 1] + 1.0)
        out[pl.ds(j, species, stride=count), :] = mean

    for i in range(4):

        @pl.when(sends[i])
        def _(i=i):
            halo_copy(i).wait_send()

    def finish(k, _):
        d = lax.rem(me + k, tiles)
        copy_of(*go, me, d, d).wait_send()
        copy_of(*back, me, d, d).wait_send()
        return 0

    lax.fori_loop(1, tiles, finish, 0)
    store.wait()


def hand_over(first, second, first_out, second_out):
    first_out[...] = first[...]
    second_out[...] = second[...]


def on_device(
    cell_means, diffusion, mix_rate, send_lists, compositions, weights, particle_slots, partners
):
    species, rows_x, rows_y, depth = cell_means.shape
    count = rows_x * rows_y
    tiles = send_lists.shape[1]
    particles = compositions.shape[1]
    blocks = particles // LANES
    vmem = lambda *shape: pltpu.VMEM(shape, F32)
    half_vmem = lambda *shape: pltpu.VMEM(shape, BF16)
    operands = (
        cell_means.reshape(species * count, depth),
        diffusion.reshape(count, depth),
        mix_rate.reshape(count, depth),
        send_lists[0],
        compositions,
        weights.reshape(blocks, LANES),
        particle_slots.reshape(blocks, LANES),
        partners.reshape(blocks, LANES),
    )
    out, new = pl.pallas_call(
        functools.partial(
            whole_kernel, lax.axis_size("gx"), lax.axis_size("gy"), rows_x, rows_y
        ),
        out_shape=(
            jax.ShapeDtypeStruct((species * count, LANES), F32),
            jax.ShapeDtypeStruct((species, particles), F32),
        ),
        in_specs=[pl.BlockSpec(memory_space=pltpu.HBM)] * 8,
        out_specs=[
            pl.BlockSpec(memory_space=pltpu.VMEM),
            pl.BlockSpec(memory_space=pltpu.HBM),
        ],
        name="whole_kernel",
        scratch_shapes=[pltpu.VMEM(a.shape, a.dtype) for a in operands]
        + [
            vmem(species, particles),
            vmem(rows_x, rows_y, ROWS, LANES),
            vmem(4, max(rows_x, rows_y), ROWS, LANES),
            vmem(count, ROWS, LANES),
            vmem(tiles, ROWS, LANES),
            vmem(tiles, ROWS, LANES),
            vmem(blocks, ROWS, LANES),
            vmem(tiles, ROWS, LANES),
            vmem(tiles, ROWS, LANES),
            half_vmem(particles // 256 * ROWS, 512),
            vmem(particles // 256 * ROWS, 256),
            vmem(ROWS, particles),
            half_vmem(ROWS, particles),
            half_vmem(ROWS, particles),
            half_vmem(256, particles),
            half_vmem(PLANE * ROWS, 1024),
            vmem(PLANE * ROWS, 256),
            half_vmem(count * ROWS, PLANE * LANES),
            vmem(count * ROWS, 256),
            pltpu.SemaphoreType.DMA((8,)),
            pltpu.SemaphoreType.DMA,
            pltpu.SemaphoreType.DMA((4,)),
            pltpu.SemaphoreType.DMA((4,)),
            pltpu.SemaphoreType.DMA((tiles,)),
            pltpu.SemaphoreType.DMA((tiles,)),
            pltpu.SemaphoreType.DMA((tiles,)),
            pltpu.SemaphoreType.DMA((tiles,)),
        ],
        compiler_params=pltpu.CompilerParams(
            collective_id=0, has_side_effects=True, vmem_limit_bytes=63 * 1024 * 1024
        ),
    )(*operands)
    out, new = pl.pallas_call(
        hand_over,
        out_shape=tuple(jax.ShapeDtypeStruct(a.shape, a.dtype) for a in (out, new)),
        in_specs=[pl.BlockSpec(memory_space=pltpu.VMEM)] * 2,
        out_specs=[pl.BlockSpec(memory_space=pltpu.VMEM)] * 2,
        name="hand_over",
    )(out, new)
    return out.reshape(species, rows_x, rows_y, depth), new


def solution(mesh):
    in_specs = (
        P(None, "gx", "gy", None),
        P("gx", "gy", None),
        P("gx", "gy", None),
        P(("gx", "gy"), None, None),
        P(None, ("gx", "gy")),
        P(("gx", "gy")),
        P(("gx", "gy")),
        P(("gx", "gy")),
    )
    out_specs = (P(None, "gx", "gy", None), P(None, ("gx", "gy")))
    return jax.shard_map(
        on_device, mesh=mesh, in_specs=in_specs, out_specs=out_specs, check_vma=False
    )
```
